32 devices in a mesh: dp: 8 (over z, x), tensor: 4 (over y, core).
Axes of the slice: x: 2, y: 2, z: 4, core: 2. Of those that a mesh axis runs over, the one named last changes fastest.
Arguments:
- layer_input: bfloat16 [4096, 768], P('dp', 'tensor'), may hold values from -6 to 6
- segment_ids: int32 [8, 512], P('dp'), may hold values from 0 to 15, never falling along the last dimension, each value on 1 to 256 neighbouring positions
- triple_weight: bfloat16 [768, 3, 768], P(None, None, 'tensor'), may hold values from -0.21875 to 0.21875
- query_value_bias: float32 [2, 768], P(None, 'tensor'), may hold values from -3 to 3
- output_weight: bfloat16 [768, 768], P('tensor'), may hold values from -0.875 to 0.875
- output_bias: float32 [768], P('tensor'), may hold values from -3 to 3
- norm_gain: float32 [768], P('tensor'), may hold values from 0.5 to 1.5
- norm_shift: float32 [768], P('tensor'), may hold values from -3 to 3
- expand_weight: bfloat16 [768, 3072], P(None, 'tensor'), may hold values from -0.21875 to 0.21875
- expand_bias: float32 [3072], P('tensor'), may hold values from -3 to 3
- reduce_weight: bfloat16 [3072, 768], P('tensor'), may hold values from -0.109375 to 0.109375
- reduce_bias: float32 [768], P('tensor'), may hold values from -3 to 3
- final_gain: float32 [768], P('tensor'), may hold values from 0.5 to 1.5
- final_shift: float32 [768], P('tensor'), may hold values from -3 to 3
- cotangent: bfloat16 [4096, 768], P('dp', 'tensor'), may hold values from -6 to 6
Outputs:
- layer_output: bfloat16 [4096, 768], P('dp', 'tensor')
- input_grad: float32 [4096, 768], P('dp', 'tensor')
- triple_grad: float32 [768, 3, 768], P(None, None, 'tensor')
- query_value_grad: float32 [2, 768], P(None, 'tensor')
- output_weight_grad: float32 [768, 768], P('tensor')
- output_bias_grad: float32 [768], P('tensor')
- norm_gain_grad: float32 [768], P('tensor')
- norm_shift_grad: float32 [768], P('tensor')
- expand_weight_grad: float32 [768, 3072], P(None, 'tensor')
- expand_bias_grad: float32 [3072], P('tensor')
- reduce_weight_grad: float32 [3072, 768], P('tensor')
- reduce_bias_grad: float32 [768], P('tensor')
- final_gain_grad: float32 [768], P('tensor')
- final_shift_grad: float32 [768], P('tensor')
The draws below stay inside these ranges and needn't reach their ends.
Inputs may be any that keep to these rules, and one draw needn't show every extreme that they name: `segment_ids`: segment numbers never fall along a sequence; each document holds 1 to 256 tokens.
All inputs are finite; a program needn't handle non-finite values.
Results may differ from the reference program's by a relative error of at most 0.012.
The reference program's roundings to bfloat16 on the way (of `probs`, `context`, `attended_half`, `activated`, `act_half`, `context_grad`, `score_grad` and `triple_half`) count: a program that leaves them out, or rounds other values in their place, can miss the bound.
Values may be sent and summed in bfloat16 or wider, within the bound.
A program may use at most 64 MiB of HBM per device.

```python
import math
import jax
import jax.numpy as jnp
import numpy as np
from jax import lax

D = 768
HEADS = 12
HD = 64
FF = 3072
SEQ_LEN = 512
DOCS = 16
SEQS = 8
TOKENS = 4096


def draw_layer_input(key, part):
    base_key = jax.random.fold_in(key, 0)
    values = jnp.clip(jax.random.normal(base_key, (TOKENS, D), jnp.float32), -6.0, 6.0)
    return values.astype(jnp.bfloat16)


def steps_of(rng, shape, cuts, smallest, top_value):
    loudness, own = 1.0, jax.random.fold_in(rng, 6)
    for position, shards_of in cuts:
        heights = jnp.exp(jax.random.uniform(jax.random.fold_in(own, position), (shards_of,), jnp.float32, smallest / len(cuts), top_value / len(cuts)))
        loudness = loudness * jnp.repeat(heights, shape[position] // shards_of).reshape([-1 if axis == position else 1 for axis in range(len(shape))])
    return loudness


def profile(amount, total, bound, skew):
    loads = [(1 << 20) // math.isqrt(grade ** skew) + 1 for grade in range(2, amount + 1)]
    rest, given = total - bound - (amount - 1), [1] * (amount - 1)
    while rest > 0:
        movable = [i for i in range(amount - 1) if given[i] < bound]
        pool, left = sum([loads[i] for i in movable]), rest
        for i in movable:
            addition = min(bound - given[i], max(1, left * loads[i] // pool), rest)
            given[i] = given[i] + addition
            rest = rest - addition
    return np.array([bound] + given)


def ragged_sizes(key, count, total, limit, lean):
    if count == 2:
        one = jax.random.randint(key, (), max(1, total - limit), min(limit, total - 1) + 1)
        return jnp.stack([one, total - one])
    tallies = jnp.asarray(profile(count, total, limit, lean), jnp.int32)
    couples = (count - 1) // 2
    source_of, sink = tallies[1:1 + 2 * couples:2], tallies[2:2 + 2 * couples:2]
    room = jnp.minimum(source_of - 1, limit - sink)
    passed = jax.random.randint(jax.random.fold_in(key, 1), (couples,), 0, 1 << 20) % (room + 1)
    tallies = tallies.at[1:1 + 2 * couples:2].set(source_of - passed).at[2:2 + 2 * couples:2].set(sink + passed)
    return tallies[jax.random.permutation(jax.random.fold_in(key, 2), count)]


def bell_draw(stream_key, extent, scale, bound, cuts=(), kind=jnp.bfloat16):
    values = jax.random.normal(stream_key, extent, jnp.float32) * scale
    if len(cuts) > 0:
        values = steps_of(stream_key, extent, cuts, -0.22, 0.18) * values
    return jnp.clip(values, min=-bound, max=bound).astype(kind)


def setup_inputs(seed: int = 0) -> dict:
    streams_of = jax.random.split(jax.random.key(seed), 16)
    return {
        "layer_input": draw_layer_input(jax.random.fold_in(streams_of[15], 71), 0),
        "segment_ids": jax.vmap(lambda own: jnp.searchsorted(jnp.cumsum(ragged_sizes(own, DOCS, SEQ_LEN, SEQ_LEN // 2, 2)), jnp.arange(SEQ_LEN), side="right"))(jax.random.split(streams_of[1], SEQS)).reshape((SEQS, SEQ_LEN)).astype(jnp.int32),
        "triple_weight": bell_draw(streams_of[2], (D, 3, D), D ** -0.5, 0.21875, ((2, 4),)),
        "query_value_bias": bell_draw(streams_of[3], (2, D), 0.5, 3.0, ((1, 4),), jnp.float32),
        "output_weight": bell_draw(streams_of[4], (D, D), (D // 16) ** -0.5, 0.875, ((0, 4),)),
        "output_bias": bell_draw(streams_of[5], (D,), 0.5, 3.0, ((0, 4),), jnp.float32),
        "norm_gain": jnp.clip(1.0 + 0.1 * jax.random.normal(streams_of[6], (D,), jnp.float32), 0.5, 1.5),
        "norm_shift": bell_draw(streams_of[7], (D,), 0.5, 3.0, ((0, 4),), jnp.float32),
        "expand_weight": bell_draw(streams_of[8], (D, FF), D ** -0.5, 0.21875, ((1, 4),)),
        "expand_bias": bell_draw(streams_of[9], (FF,), 0.5, 3.0, ((0, 4),), jnp.float32),
        "reduce_weight": bell_draw(streams_of[10], (FF, D), FF ** -0.5, 0.109375, ((0, 4),)),
        "reduce_bias": bell_draw(streams_of[11], (D,), 0.5, 3.0, ((0, 4),), jnp.float32),
        "final_gain": jnp.clip(1.0 + 0.1 * jax.random.normal(streams_of[12], (D,), jnp.float32), 0.5, 1.5),
        "final_shift": bell_draw(streams_of[13], (D,), 0.5, 3.0, ((0, 4),), jnp.float32),
        "cotangent": bell_draw(streams_of[14], (TOKENS, D), 1.0, 6.0, ((0, 8), (1, 4))),
    }


EPS = 1e-06

def gelu_value(pre_act):
    return 0.5 * pre_act * (1.0 + lax.erf(pre_act * 0.7071067811865476))

def gelu_slope(pre_act):
    return 0.5 * (1.0 + lax.erf(pre_act * 0.7071067811865476)) + pre_act * jnp.exp(-0.5 * pre_act * pre_act) * 0.3989422804014327

def norm_forward(hidden, gain, shift):
    row_mean = lax.optimization_barrier(jnp.mean(hidden, axis=-1, keepdims=True))
    centred = hidden - row_mean
    inverse = lax.rsqrt(lax.optimization_barrier(jnp.mean(centred * centred, axis=-1, keepdims=True)) + EPS)
    normed = centred * inverse
    return (normed * gain + shift, normed, inverse)

def norm_backward(upstream, normed, inverse, gain):
    scaled = upstream * gain
    return inverse * (scaled - lax.optimization_barrier(jnp.mean(scaled, axis=-1, keepdims=True)) - normed * lax.optimization_barrier(jnp.mean(scaled * normed, axis=-1, keepdims=True)))

def fdot(left, right):
    return jnp.dot(left, right, preferred_element_type=jnp.float32)

def tdot(left, right):
    return jnp.dot(left.astype(jnp.float32).T, right.astype(jnp.float32))

def one_sequence(params, seq_input, seq_segments, seq_cot):
    triple_weight, query_value_bias, output_weight, output_bias, norm_gain, norm_shift, expand_weight, expand_bias, reduce_weight, reduce_bias, final_gain, final_shift = params
    seq_len = seq_input.shape[0]
    head_scale = HD ** (-0.5)
    input_f = seq_input.astype(jnp.float32)
    projected = jnp.einsum('ld,dcf->lcf', input_f, triple_weight.astype(jnp.float32))
    queries = (projected[:, 0] + query_value_bias[0]).astype(jnp.bfloat16).reshape(seq_len, HEADS, HD)
    keys_half = projected[:, 1].astype(jnp.bfloat16).reshape(seq_len, HEADS, HD)
    values = (projected[:, 2] + query_value_bias[1]).astype(jnp.bfloat16).reshape(seq_len, HEADS, HD)
    allowed = seq_segments[:, None] == seq_segments[None, :]
    scores = jnp.einsum('qhd,khd->hqk', queries.astype(jnp.float32), keys_half.astype(jnp.float32)) * head_scale
    scores = jnp.where(allowed[None], scores, -jnp.inf)
    top = lax.optimization_barrier(jnp.max(scores, axis=-1, keepdims=True))
    log_total = top + jnp.log(lax.optimization_barrier(jnp.sum(jnp.exp(scores - top), axis=-1, keepdims=True)))
    probs = jnp.exp(scores - log_total)
    probs_half = probs.astype(jnp.bfloat16)
    context = jnp.einsum('hqk,khd->qhd', probs_half.astype(jnp.float32), values.astype(jnp.float32)).astype(jnp.bfloat16)
    context_flat = context.reshape(seq_len, D)
    first_sum = input_f + fdot(context_flat, output_weight) + output_bias
    attended, normed_one, inv_one = norm_forward(first_sum, norm_gain, norm_shift)
    attended_half = attended.astype(jnp.bfloat16)
    pre_act = fdot(attended_half, expand_weight) + expand_bias
    activated = gelu_value(pre_act).astype(jnp.bfloat16)
    second_sum = attended + fdot(activated, reduce_weight) + reduce_bias
    out_f, normed_two, inv_two = norm_forward(second_sum, final_gain, final_shift)
    layer_output = out_f.astype(jnp.bfloat16)
    upstream = seq_cot.astype(jnp.float32)
    final_gain_grad = lax.optimization_barrier(jnp.sum(upstream * normed_two, axis=0))
    final_shift_grad = lax.optimization_barrier(jnp.sum(upstream, axis=0))
    second_grad = norm_backward(upstream, normed_two, inv_two, final_gain)
    second_half = second_grad.astype(jnp.bfloat16)
    reduce_weight_grad = tdot(activated, second_half)
    reduce_bias_grad = lax.optimization_barrier(jnp.sum(second_grad, axis=0))
    act_grad = jnp.dot(second_half.astype(jnp.float32), reduce_weight.astype(jnp.float32).T) * gelu_slope(pre_act)
    act_half = act_grad.astype(jnp.bfloat16)
    expand_weight_grad = tdot(attended_half, act_half)
    expand_bias_grad = lax.optimization_barrier(jnp.sum(act_grad, axis=0))
    attended_grad = second_grad + jnp.dot(act_half.astype(jnp.float32), expand_weight.astype(jnp.float32).T)
    norm_gain_grad = lax.optimization_barrier(jnp.sum(attended_grad * normed_one, axis=0))
    norm_shift_grad = lax.optimization_barrier(jnp.sum(attended_grad, axis=0))
    first_grad = norm_backward(attended_grad, normed_one, inv_one, norm_gain)
    first_half = first_grad.astype(jnp.bfloat16)
    output_weight_grad = tdot(context_flat, first_half)
    output_bias_grad = lax.optimization_barrier(jnp.sum(first_grad, axis=0))
    context_grad = jnp.dot(first_half.astype(jnp.float32), output_weight.astype(jnp.float32).T).astype(jnp.bfloat16)
    context_grad = context_grad.reshape(seq_len, HEADS, HD)
    probs_again = jnp.exp(scores - log_total)
    cg_f = context_grad.astype(jnp.float32)
    value_grad = jnp.einsum('hqk,qhd->khd', probs_half.astype(jnp.float32), cg_f)
    prob_grad = jnp.einsum('qhd,khd->hqk', cg_f, values.astype(jnp.float32))
    delta = jnp.einsum('qhd,qhd->hq', cg_f, context.astype(jnp.float32))
    score_grad = (probs_again * (prob_grad - delta[:, :, None]) * head_scale).astype(jnp.bfloat16).astype(jnp.float32)
    query_grad = jnp.einsum('hqk,khd->qhd', score_grad, keys_half.astype(jnp.float32)).reshape(seq_len, D)
    key_grad = jnp.einsum('hqk,qhd->khd', score_grad, queries.astype(jnp.float32)).reshape(seq_len, D)
    value_grad = value_grad.reshape(seq_len, D)
    query_value_grad = jnp.stack([lax.optimization_barrier(jnp.sum(query_grad, axis=0)), lax.optimization_barrier(jnp.sum(value_grad, axis=0))])
    triple_half = jnp.stack([query_grad, key_grad, value_grad], axis=1).astype(jnp.bfloat16).astype(jnp.float32)
    triple_grad = jnp.einsum('ld,lcf->dcf', input_f, triple_half)
    input_grad = first_grad + jnp.einsum('lcf,dcf->ld', triple_half, triple_weight.astype(jnp.float32))
    grads = (triple_grad, query_value_grad, output_weight_grad, output_bias_grad, norm_gain_grad, norm_shift_grad, expand_weight_grad, expand_bias_grad, reduce_weight_grad, reduce_bias_grad, final_gain_grad, final_shift_grad)
    return (layer_output, input_grad, grads)

def reference(layer_input, segment_ids, triple_weight, query_value_bias, output_weight, output_bias, norm_gain, norm_shift, expand_weight, expand_bias, reduce_weight, reduce_bias, final_gain, final_shift, cotangent):
    params = (triple_weight, query_value_bias, output_weight, output_bias, norm_gain, norm_shift, expand_weight, expand_bias, reduce_weight, reduce_bias, final_gain, final_shift)
    seq_count = segment_ids.shape[0]
    seq_len = segment_ids.shape[1]
    inputs_by_seq = layer_input.reshape(seq_count, seq_len, D)
    cots_by_seq = cotangent.reshape(seq_count, seq_len, D)
    zeros = tuple((jnp.zeros(p.shape, jnp.float32) for p in params))

    def step_fn(carry, items):
        seq_input, seq_segments, seq_cot = items
        out_rows, grad_rows, grads = one_sequence(params, seq_input, seq_segments, seq_cot)
        carry = tuple((c + g for c, g in zip(carry, grads)))
        return (carry, (out_rows, grad_rows))
    totals, (outputs, input_grads) = lax.scan(step_fn, zeros, (inputs_by_seq, segment_ids, cots_by_seq))
    layer_output = outputs.reshape(seq_count * seq_len, D)
    input_grad = input_grads.reshape(seq_count * seq_len, D)
    return (layer_output, input_grad, totals[0], totals[1], totals[2], totals[3], totals[4], totals[5], totals[6], totals[7], totals[8], totals[9], totals[10], totals[11])
```

```python
import jax
import jax.numpy as jnp
from jax import lax
from jax.sharding import PartitionSpec as P

D = 768
HD = 64


EPS = 1e-06


def gelu_value(pre_act):
    return 0.5 * pre_act * (1.0 + lax.erf(pre_act * 0.7071067811865476))


def gelu_slope(pre_act):
    return (
        0.5 * (1.0 + lax.erf(pre_act * 0.7071067811865476))
        + pre_act * jnp.exp(-0.5 * pre_act * pre_act) * 0.3989422804014327
    )


def norm_forward(hidden, gain, shift):
    row_mean = jnp.mean(hidden, axis=-1, keepdims=True)
    centred = hidden - row_mean
    inverse = lax.rsqrt(jnp.mean(centred * centred, axis=-1, keepdims=True) + EPS)
    normed = centred * inverse
    return (normed * gain + shift, normed, inverse)


def norm_backward(upstream, normed, inverse, gain):
    scaled = upstream * gain
    first_mean = jnp.mean(scaled, axis=-1, keepdims=True)
    second_mean = jnp.mean(scaled * normed, axis=-1, keepdims=True)
    return inverse * (scaled - first_mean - normed * second_mean)


def sum_rows(partial):
    return lax.psum_scatter(
        partial.astype(jnp.bfloat16), "tensor", scatter_dimension=0, tiled=True
    ).astype(jnp.float32)


def all_rows(piece):
    return lax.all_gather(piece, "tensor", axis=0, tiled=True)


def column_sum(rows):
    return jnp.sum(rows, axis=0)


def tall_dot(left, right):
    return lax.dot_general(
        left, right, (((0,), (0,)), ((), ())), preferred_element_type=jnp.float32
    )


def wide_dot(left, right):
    return lax.dot_general(
        left, right, (((1,), (1,)), ((), ())), preferred_element_type=jnp.float32
    )


def masked_scores(query_part, key_part, segment_row, head_scale):
    scores = (
        jnp.einsum("qhd,khd->hqk", query_part, key_part, preferred_element_type=jnp.float32)
        * head_scale
    )
    allowed = segment_row[:, None] == segment_row[None, :]
    return jnp.where(allowed[None], scores, -jnp.inf)


def per_device(
    layer_input,
    segment_ids,
    triple_weight,
    query_value_bias,
    output_weight,
    output_bias,
    norm_gain,
    norm_shift,
    expand_weight,
    expand_bias,
    reduce_weight,
    reduce_bias,
    final_gain,
    final_shift,
    cotangent,
):
    seq_len = segment_ids.shape[1]
    tok_count = segment_ids.shape[0] * seq_len
    local_width = triple_weight.shape[2]
    local_heads = local_width // HD
    head_scale = HD ** (-0.5)
    groups = lax.axis_size("tensor")
    rank = lax.axis_index("tensor")
    block = tok_count // groups
    both = lax.all_gather(
        jnp.concatenate([layer_input, cotangent], axis=0), "tensor", axis=1, tiled=True
    )
    gathered = both[:tok_count]
    own_input = lax.dynamic_slice_in_dim(both, rank * block, block, 0).astype(jnp.float32)
    upstream = lax.dynamic_slice_in_dim(both, tok_count + rank * block, block, 0).astype(
        jnp.float32
    )
    vectors = lax.all_gather(
        jnp.stack([output_bias, norm_gain, norm_shift, reduce_bias, final_gain, final_shift]),
        "tensor",
        axis=1,
        tiled=True,
    )
    output_bias, norm_gain, norm_shift, reduce_bias, final_gain, final_shift = [
        vectors[i] for i in range(6)
    ]
    projected = jnp.einsum(
        "td,dcf->tcf", gathered, triple_weight, preferred_element_type=jnp.float32
    )
    query_half = (
        (projected[:, 0] + query_value_bias[0])
        .astype(jnp.bfloat16)
        .reshape(seq_len, local_heads, HD)
    )
    key_half = projected[:, 1].astype(jnp.bfloat16).reshape(seq_len, local_heads, HD)
    value_half = (
        (projected[:, 2] + query_value_bias[1])
        .astype(jnp.bfloat16)
        .reshape(seq_len, local_heads, HD)
    )
    scores = masked_scores(query_half, key_half, segment_ids[0], head_scale)
    top = jnp.max(scores, axis=-1, keepdims=True)
    log_total = top + jnp.log(jnp.sum(jnp.exp(scores - top), axis=-1, keepdims=True))
    probs_half = jnp.exp(scores - log_total).astype(jnp.bfloat16)
    context = jnp.einsum(
        "hqk,khd->qhd", probs_half, value_half, preferred_element_type=jnp.float32
    ).astype(jnp.bfloat16)
    context_flat = context.reshape(tok_count, local_width)
    first_sum = (
        own_input
        + sum_rows(jnp.dot(context_flat, output_weight, preferred_element_type=jnp.float32))
        + output_bias
    )
    attended, normed_one, inv_one = norm_forward(first_sum, norm_gain, norm_shift)
    attended_half = all_rows(attended.astype(jnp.bfloat16))
    pre_act = (
        jnp.dot(attended_half, expand_weight, preferred_element_type=jnp.float32) + expand_bias
    )
    activated = gelu_value(pre_act).astype(jnp.bfloat16)
    second_sum = (
        attended
        + sum_rows(jnp.dot(activated, reduce_weight, preferred_element_type=jnp.float32))
        + reduce_bias
    )
    out_f, normed_two, inv_two = norm_forward(second_sum, final_gain, final_shift)
    layer_output = lax.all_to_all(
        out_f.astype(jnp.bfloat16), "tensor", split_axis=1, concat_axis=0, tiled=True
    )
    final_gain_grad = column_sum(upstream * normed_two)
    final_shift_grad = column_sum(upstream)
    second_grad = norm_backward(upstream, normed_two, inv_two, final_gain)
    second_half = all_rows(second_grad.astype(jnp.bfloat16))
    reduce_weight_grad = tall_dot(activated, second_half)
    reduce_bias_grad = column_sum(second_grad)
    act_grad = wide_dot(second_half, reduce_weight) * gelu_slope(pre_act)
    act_half = act_grad.astype(jnp.bfloat16)
    expand_weight_grad = tall_dot(attended_half, act_half)
    expand_bias_grad = column_sum(act_grad)
    feed_sum = lax.psum(
        jnp.concatenate([reduce_weight_grad, expand_weight_grad], axis=0).astype(jnp.bfloat16),
        "dp",
    )
    split = reduce_weight_grad.shape[0]
    attended_grad = second_grad + sum_rows(wide_dot(act_half, expand_weight))
    norm_gain_grad = column_sum(attended_grad * normed_one)
    norm_shift_grad = column_sum(attended_grad)
    first_grad = norm_backward(attended_grad, normed_one, inv_one, norm_gain)
    first_half = all_rows(first_grad.astype(jnp.bfloat16))
    output_weight_grad = tall_dot(context_flat, first_half)
    output_bias_grad = column_sum(first_grad)
    grad_part = (
        wide_dot(first_half, output_weight)
        .astype(jnp.bfloat16)
        .reshape(seq_len, local_heads, HD)
    )
    scores = masked_scores(query_half, key_half, segment_ids[0], head_scale)
    probs = jnp.exp(scores - log_total)
    probs_half = probs.astype(jnp.bfloat16)
    value_grad = jnp.einsum(
        "hqk,qhd->khd", probs_half, grad_part, preferred_element_type=jnp.float32
    ).reshape(tok_count, local_width)
    prob_grad = jnp.einsum(
        "qhd,khd->hqk", grad_part, value_half, preferred_element_type=jnp.float32
    )
    delta = jnp.einsum(
        "qhd,qhd->hq", grad_part.astype(jnp.float32), context.astype(jnp.float32)
    )
    score_grad = (probs * (prob_grad - delta[:, :, None]) * head_scale).astype(jnp.bfloat16)
    query_grad = jnp.einsum(
        "hqk,khd->qhd", score_grad, key_half, preferred_element_type=jnp.float32
    ).reshape(tok_count, local_width)
    key_grad = jnp.einsum(
        "hqk,qhd->khd", score_grad, query_half, preferred_element_type=jnp.float32
    ).reshape(tok_count, local_width)
    triple_half = jnp.stack([query_grad, key_grad, value_grad], axis=1).astype(jnp.bfloat16)
    triple_grad = jnp.einsum(
        "td,tcf->dcf", gathered, triple_half, preferred_element_type=jnp.float32
    )
    input_terms = jnp.einsum(
        "tcf,dcf->td", triple_half, triple_weight, preferred_element_type=jnp.float32
    )
    smalls = jnp.stack(
        [
            output_bias_grad,
            norm_gain_grad,
            norm_shift_grad,
            reduce_bias_grad,
            final_gain_grad,
            final_shift_grad,
        ]
    )
    own_rows = lax.dynamic_slice_in_dim(input_terms, rank * block, block, 0) + first_grad
    input_terms = lax.dynamic_update_slice_in_dim(input_terms, own_rows, rank * block, 0)
    shares = lax.psum_scatter(
        jnp.concatenate([input_terms, smalls, jnp.zeros((10, D), jnp.float32)], axis=0).astype(jnp.bfloat16),
        "tensor",
        scatter_dimension=1,
        tiled=True,
    ).astype(jnp.float32)
    input_grad = shares[:tok_count]
    pieces = [
        triple_grad,
        output_weight_grad,
        expand_bias_grad,
        jnp.sum(query_grad, axis=0),
        jnp.sum(value_grad, axis=0),
        shares[tok_count : tok_count + 6],
    ]
    packed = jnp.concatenate([p.reshape(-1, local_width) for p in pieces], axis=0)
    packed, feed_sum = lax.optimization_barrier((packed.astype(jnp.bfloat16), feed_sum))
    packed = lax.psum(packed, "dp").astype(jnp.float32)
    reduce_weight_grad = feed_sum[:split].astype(jnp.float32)
    expand_weight_grad = feed_sum[split:].astype(jnp.float32)
    outs, at = [], 0
    for p in pieces:
        count = p.size // local_width
        outs.append(packed[at : at + count].reshape(p.shape))
        at += count
    triple_grad, output_weight_grad, expand_bias_grad, query_sum, value_sum, small_sums = outs
    return (
        layer_output,
        input_grad,
        triple_grad,
        jnp.stack([query_sum, value_sum]),
        output_weight_grad,
        small_sums[0],
        small_sums[1],
        small_sums[2],
        expand_weight_grad,
        expand_bias_grad,
        reduce_weight_grad,
        small_sums[3],
        small_sums[4],
        small_sums[5],
    )


def solution(mesh):
    in_specs = (
        P("dp", "tensor"),
        P("dp", None),
        P(None, None, "tensor"),
        P(None, "tensor"),
        P("tensor", None),
        P("tensor"),
        P("tensor"),
        P("tensor"),
        P(None, "tensor"),
        P("tensor"),
        P("tensor", None),
        P("tensor"),
        P("tensor"),
        P("tensor"),
        P("dp", "tensor"),
    )
    out_specs = (
        P("dp", "tensor"),
        P("dp", "tensor"),
        P(None, None, "tensor"),
        P(None, "tensor"),
        P("tensor", None),
        P("tensor"),
        P("tensor"),
        P("tensor"),
        P(None, "tensor"),
        P("tensor"),
        P("tensor", None),
        P("tensor"),
        P("tensor"),
        P("tensor"),
    )
    return jax.shard_map(
        per_device, mesh=mesh, in_specs=in_specs, out_specs=out_specs, check_vma=False
    )
```

```python
import jax
import jax.numpy as jnp
from jax import lax
from jax.experimental import pallas as pl
from jax.experimental.pallas import tpu as pltpu
from jax.sharding import PartitionSpec as P

D = 768
HD = 64


EPS = 1e-06


def gelu_value(pre_act):
    return 0.5 * pre_act * (1.0 + lax.erf(pre_act * 0.7071067811865476))


def gelu_slope(pre_act):
    return (
        0.5 * (1.0 + lax.erf(pre_act * 0.7071067811865476))
        + pre_act * jnp.exp(-0.5 * pre_act * pre_act) * 0.3989422804014327
    )


def norm_forward(hidden, gain, shift):
    row_mean = jnp.mean(hidden, axis=-1, keepdims=True)
    centred = hidden - row_mean
    inverse = lax.rsqrt(jnp.mean(centred * centred, axis=-1, keepdims=True) + EPS)
    normed = centred * inverse
    return (normed * gain + shift, normed, inverse)


def norm_backward(upstream, normed, inverse, gain):
    scaled = upstream * gain
    first_mean = jnp.mean(scaled, axis=-1, keepdims=True)
    second_mean = jnp.mean(scaled * normed, axis=-1, keepdims=True)
    return inverse * (scaled - first_mean - normed * second_mean)


VMEM = pl.BlockSpec(memory_space=pltpu.VMEM)


def greet(peers):
    barrier = pltpu.get_barrier_semaphore()
    for peer in peers:
        pl.semaphore_signal(
            barrier,
            inc=1,
            device_id=(lax.axis_index("dp"), peer),
            device_id_type=pl.DeviceIdType.MESH,
        )
    pl.semaphore_wait(barrier, len(peers))


def remote(src, dst, sems, slot, peer):
    copy = pltpu.make_async_remote_copy(
        src_ref=src,
        dst_ref=dst,
        send_sem=sems[0].at[slot],
        recv_sem=sems[1].at[slot],
        device_id=(lax.axis_index("dp"), peer),
        device_id_type=pl.DeviceIdType.MESH,
    )
    copy.start()
    return copy


def call(body, identity, outs, scratch, copies, args):
    return pl.pallas_call(
        body,
        out_shape=outs,
        in_specs=[VMEM] * len(args),
        out_specs=[VMEM] * len(outs),
        scratch_shapes=scratch
        + [pltpu.SemaphoreType.DMA((copies,)), pltpu.SemaphoreType.DMA((copies,))],
        compiler_params=pltpu.CompilerParams(
            collective_id=identity, has_side_effects=True, vmem_limit_bytes=40 << 20
        ),
    )(*args)


def sum_norm_gather(identity, step, partial, aux, outs):
    rows, width = partial.shape
    block = rows // 4
    count = len(aux)

    def body(*refs):
        part, ins = refs[0], refs[1 : 1 + count]
        full, results = refs[1 + count], refs[2 + count : 2 + count + len(outs)]
        near, held, far = refs[-5:-2]
        sems = refs[-2:]
        me = lax.axis_index("tensor")
        core, chip = me % 2, me // 2
        mate = chip * 2 + 1 - core
        across = (1 - chip) * 2 + core

        def at(owner):
            return pl.ds(pl.multiple_of(owner * block, block), block)

        greet((mate, across))
        diagonal = (1 - chip) * 2 + 1 - core
        one = remote(part.at[at(diagonal)], near.at[0], sems, 0, mate)
        two = remote(part.at[at(mate)], near.at[1], sems, 1, mate)
        one.wait()
        held[...] = (
            part[at(across), :].astype(jnp.float32) + near[0].astype(jnp.float32)
        ).astype(jnp.bfloat16)
        three = remote(held, far, sems, 2, across)
        two.wait()
        total = part[at(me), :].astype(jnp.float32) + near[1].astype(jnp.float32)
        three.wait()
        values = step(total + far[...].astype(jnp.float32), *[ref[...] for ref in ins])
        full[at(me), :] = values[0].astype(jnp.bfloat16)
        four = remote(full.at[at(me)], full.at[at(me)], sems, 3, across)
        five = remote(full.at[at(me)], full.at[at(me)], sems, 4, mate)
        for ref, value in zip(results, values[1:]):
            ref[...] = value.astype(ref.dtype)
        four.wait()
        six = remote(full.at[at(across)], full.at[at(across)], sems, 5, mate)
        five.wait()
        six.wait()

    return call(
        body,
        identity,
        [jax.ShapeDtypeStruct((rows, width), jnp.bfloat16)] + outs,
        [
            pltpu.VMEM((2, block, width), jnp.bfloat16),
            pltpu.VMEM((block, width), jnp.bfloat16),
            pltpu.VMEM((block, width), jnp.bfloat16),
        ],
        6,
        [partial] + aux,
    )


def gather_inputs(layer_input, cotangent, vectors):
    rows, width = layer_input.shape
    block = rows // 4

    def body(x_ref, c_ref, v_ref, x_out, c_out, v_out, *sems):
        me = lax.axis_index("tensor")
        peers = [lax.rem(me + d, 4) for d in (1, 2, 3)]
        greet(peers)
        copies = []
        for i, peer in enumerate(peers):
            copies.append(remote(x_ref, x_out.at[me], sems, 3 * i, peer))
            copies.append(remote(v_ref, v_out.at[me], sems, 3 * i + 1, peer))
            src = c_ref.at[pl.ds(pl.multiple_of(peer * block, block), block)]
            copies.append(remote(src, c_out.at[me], sems, 3 * i + 2, peer))
        x_out[me] = x_ref[...]
        v_out[me] = v_ref[...]
        c_out[me] = c_ref[pl.ds(pl.multiple_of(me * block, block), block), :]
        for copy in copies:
            copy.wait()

    return call(
        body,
        0,
        [
            jax.ShapeDtypeStruct((4, rows, width), layer_input.dtype),
            jax.ShapeDtypeStruct((4, block, width), cotangent.dtype),
            jax.ShapeDtypeStruct((4,) + vectors.shape, vectors.dtype),
        ],
        [],
        9,
        [layer_input, cotangent, vectors],
    )


def scatter_outputs(terms, rows_out):
    _, rows, width = terms.shape
    block = rows_out.shape[1]

    def body(t_ref, o_ref, sum_ref, o_out, held, *sems):
        me = lax.axis_index("tensor")
        peers = [lax.rem(me + d, 4) for d in (1, 2, 3)]
        greet(peers)
        copies = []
        for i, peer in enumerate(peers):
            copies.append(remote(t_ref.at[peer], held.at[i], sems, 2 * i, peer))
        for i, peer in enumerate(peers):
            copies.append(remote(o_ref.at[peer], o_out.at[me], sems, 2 * i + 1, peer))
        o_out[me] = o_ref[me]
        total = t_ref[me].astype(jnp.float32)
        for i in range(3):
            copies[i].wait()
            total = total + held[i].astype(jnp.float32)
        sum_ref[...] = total
        for copy in copies[3:]:
            copy.wait()

    return call(
        body,
        1,
        [
            jax.ShapeDtypeStruct((rows, width), jnp.float32),
            jax.ShapeDtypeStruct(rows_out.shape, rows_out.dtype),
        ],
        [pltpu.VMEM((3, rows, width), terms.dtype)],
        6,
        [terms, rows_out],
    )


def swap(piece, bit):
    size = lax.axis_size("dp")
    return lax.ppermute(piece, "dp", [(i, i ^ bit) for i in range(size)])


def added(left, right):
    return (left.astype(jnp.float32) + right.astype(jnp.float32)).astype(jnp.bfloat16)


def dp_sum(piece, turn):
    bits = [1 << i for i in range(lax.axis_size("dp").bit_length() - 1)]
    bits = bits[turn:] + bits[:turn]
    me = lax.axis_index("dp")
    piece = piece.astype(jnp.bfloat16)
    for bit in bits:
        upper = (me // bit) % 2 == 1
        half = piece.shape[0] // 2
        low, high = piece[:half], piece[half:]
        other = swap(jnp.where(upper, low, high), bit)
        piece = added(jnp.where(upper, high, low), other)
    for bit in reversed(bits):
        upper = (me // bit) % 2 == 1
        other = swap(piece, bit)
        piece = jnp.concatenate(
            [jnp.where(upper, other, piece), jnp.where(upper, piece, other)], axis=0
        )
    return piece.astype(jnp.float32)


def dp_sum_small(piece):
    for i in range(lax.axis_size("dp").bit_length() - 1):
        piece = piece + swap(piece, 1 << i)
    return piece


def column_sum(rows):
    return jnp.sum(rows, axis=0, keepdims=True)


def tall_dot(left, right):
    return lax.dot_general(
        left, right, (((0,), (0,)), ((), ())), preferred_element_type=jnp.float32
    )


def wide_dot(left, right):
    return lax.dot_general(
        left, right, (((1,), (1,)), ((), ())), preferred_element_type=jnp.float32
    )


def masked_scores(query_part, key_part, segment_row, head_scale):
    scores = (
        jnp.einsum("qhd,khd->hqk", query_part, key_part, preferred_element_type=jnp.float32)
        * head_scale
    )
    allowed = segment_row[:, None] == segment_row[None, :]
    return jnp.where(allowed[None], scores, -jnp.inf)


def per_device(
    layer_input,
    segment_ids,
    triple_weight,
    query_value_bias,
    output_weight,
    output_bias,
    norm_gain,
    norm_shift,
    expand_weight,
    expand_bias,
    reduce_weight,
    reduce_bias,
    final_gain,
    final_shift,
    cotangent,
):
    seq_len = segment_ids.shape[1]
    tok_count = segment_ids.shape[0] * seq_len
    local_width = triple_weight.shape[2]
    local_heads = local_width // HD
    head_scale = HD ** (-0.5)
    rank = lax.axis_index("tensor")
    block = tok_count // 4
    stacked = jnp.stack(
        [output_bias, norm_gain, norm_shift, reduce_bias, final_gain, final_shift] + [final_shift] * 2
    )
    x_all, c_all, v_all = gather_inputs(layer_input, cotangent, stacked)
    gathered = jnp.concatenate([x_all[i] for i in range(4)], axis=1)
    cot_own = jnp.concatenate([c_all[i] for i in range(4)], axis=1)
    vectors = jnp.concatenate([v_all[i] for i in range(4)], axis=1)
    input_own = lax.dynamic_slice_in_dim(gathered, rank * block, block, 0)
    wide = jax.ShapeDtypeStruct((block, D), jnp.float32)
    narrow = jax.ShapeDtypeStruct((block, 1), jnp.float32)
    line = jax.ShapeDtypeStruct((1, D), jnp.float32)
    half_wide = jax.ShapeDtypeStruct((block, D), jnp.bfloat16)

    def first_step(total, own, vec):
        hidden = own.astype(jnp.float32) + total + vec[0:1]
        attended, normed, inverse = norm_forward(hidden, vec[1:2], vec[2:3])
        return attended, attended, normed, inverse

    def second_step(total, attended, cot, vec):
        hidden = attended + total + vec[3:4]
        out, normed, inverse = norm_forward(hidden, vec[4:5], vec[5:6])
        upstream = cot.astype(jnp.float32)
        grad = norm_backward(upstream, normed, inverse, vec[4:5])
        return (
            grad,
            grad,
            out,
            column_sum(upstream * normed),
            column_sum(upstream),
            column_sum(grad),
        )

    def third_step(total, second_grad, normed, inverse, vec):
        grad_in = second_grad + total
        grad = norm_backward(grad_in, normed, inverse, vec[1:2])
        return (
            grad,
            grad,
            column_sum(grad_in * normed),
            column_sum(grad_in),
            column_sum(grad),
        )

    projected = jnp.einsum(
        "td,dcf->tcf", gathered, triple_weight, preferred_element_type=jnp.float32
    )
    query_half = (
        (projected[:, 0] + query_value_bias[0])
        .astype(jnp.bfloat16)
        .reshape(seq_len, local_heads, HD)
    )
    key_half = projected[:, 1].astype(jnp.bfloat16).reshape(seq_len, local_heads, HD)
    value_half = (
        (projected[:, 2] + query_value_bias[1])
        .astype(jnp.bfloat16)
        .reshape(seq_len, local_heads, HD)
    )
    scores = masked_scores(query_half, key_half, segment_ids[0], head_scale)
    top = jnp.max(scores, axis=-1, keepdims=True)
    log_total = top + jnp.log(jnp.sum(jnp.exp(scores - top), axis=-1, keepdims=True))
    probs_half = jnp.exp(scores - log_total).astype(jnp.bfloat16)
    context = jnp.einsum(
        "hqk,khd->qhd", probs_half, value_half, preferred_element_type=jnp.float32
    ).astype(jnp.bfloat16)
    context_flat = context.reshape(tok_count, local_width)
    attended_half, attended, normed_one, inv_one = sum_norm_gather(
        2,
        first_step,
        jnp.dot(context_flat, output_weight, preferred_element_type=jnp.float32).astype(
            jnp.bfloat16
        ),
        [input_own, vectors],
        [wide, wide, narrow],
    )
    pre_act = (
        jnp.dot(attended_half, expand_weight, preferred_element_type=jnp.float32) + expand_bias
    )
    activated = gelu_value(pre_act).astype(jnp.bfloat16)
    second_half, second_grad, out_rows, final_gain_grad, final_shift_grad, reduce_bias_grad = (
        sum_norm_gather(
            3,
            second_step,
            jnp.dot(activated, reduce_weight, preferred_element_type=jnp.float32).astype(
                jnp.bfloat16
            ),
            [attended, cot_own, vectors],
            [wide, half_wide, line, line, line],
        )
    )
    reduce_weight_grad = tall_dot(activated, second_half)
    act_grad = wide_dot(second_half, reduce_weight) * gelu_slope(pre_act)
    act_half = act_grad.astype(jnp.bfloat16)
    expand_weight_grad = tall_dot(attended_half, act_half)
    expand_bias_grad = jnp.sum(act_grad, axis=0)
    reduce_weight_grad = dp_sum(reduce_weight_grad, 0)
    expand_weight_grad = dp_sum(expand_weight_grad, 1)
    first_half, first_grad, norm_gain_grad, norm_shift_grad, output_bias_grad = sum_norm_gather(
        4,
        third_step,
        wide_dot(act_half, expand_weight).astype(jnp.bfloat16),
        [second_grad, normed_one, inv_one, vectors],
        [wide, line, line, line],
    )
    output_weight_grad = tall_dot(context_flat, first_half)
    output_weight_grad = dp_sum(output_weight_grad, 0)
    grad_part = (
        wide_dot(first_half, output_weight)
        .astype(jnp.bfloat16)
        .reshape(seq_len, local_heads, HD)
    )
    scores = masked_scores(query_half, key_half, segment_ids[0], head_scale)
    probs = jnp.exp(scores - log_total)
    probs_half = probs.astype(jnp.bfloat16)
    value_grad = jnp.einsum(
        "hqk,qhd->khd", probs_half, grad_part, preferred_element_type=jnp.float32
    ).reshape(tok_count, local_width)
    prob_grad = jnp.einsum(
        "qhd,khd->hqk", grad_part, value_half, preferred_element_type=jnp.float32
    )
    delta = jnp.einsum(
        "qhd,qhd->hq", grad_part.astype(jnp.float32), context.astype(jnp.float32)
    )
    score_grad = (probs * (prob_grad - delta[:, :, None]) * head_scale).astype(jnp.bfloat16)
    query_grad = jnp.einsum(
        "hqk,khd->qhd", score_grad, key_half, preferred_element_type=jnp.float32
    ).reshape(tok_count, local_width)
    key_grad = jnp.einsum(
        "hqk,qhd->khd", score_grad, query_half, preferred_element_type=jnp.float32
    ).reshape(tok_count, local_width)
    triple_half = jnp.stack([query_grad, key_grad, value_grad], axis=1).astype(jnp.bfloat16)
    triple_grad = jnp.einsum(
        "td,tcf->dcf", gathered, triple_half, preferred_element_type=jnp.float32
    )
    flat = triple_grad.reshape(D, -1)
    triple_grad = jnp.concatenate(
        [dp_sum(flat[: D // 2], 0), dp_sum(flat[D // 2 :], 1)], axis=0
    ).reshape(triple_grad.shape)
    input_terms = jnp.einsum(
        "tcf,dcf->td", triple_half, triple_weight, preferred_element_type=jnp.float32
    )
    smalls = jnp.concatenate(
        [
            output_bias_grad,
            norm_gain_grad,
            norm_shift_grad,
            reduce_bias_grad,
            final_gain_grad,
            final_shift_grad,
            jnp.zeros((10, D), jnp.float32),
        ],
        axis=0,
    )
    own_rows = lax.dynamic_slice_in_dim(input_terms, rank * block, block, 0) + first_grad
    input_terms = lax.dynamic_update_slice_in_dim(input_terms, own_rows, rank * block, 0)
    terms = jnp.concatenate([input_terms, smalls], axis=0).astype(jnp.bfloat16)
    shares, layer_output = scatter_outputs(
        jnp.stack(jnp.split(terms, 4, axis=1)), jnp.stack(jnp.split(out_rows, 4, axis=1))
    )
    layer_output = layer_output.reshape(tok_count, local_width)
    input_grad = shares[:tok_count]
    packed = jnp.concatenate(
        [
            expand_bias_grad.reshape(-1, local_width),
            jnp.sum(query_grad, axis=0, keepdims=True),
            jnp.sum(value_grad, axis=0, keepdims=True),
            shares[tok_count : tok_count + 6],
        ],
        axis=0,
    )
    packed = dp_sum_small(packed)
    extra = packed.shape[0] - 8
    expand_bias_grad = packed[:extra].reshape(-1)
    query_sum, value_sum = packed[extra], packed[extra + 1]
    small_sums = packed[extra + 2 :]
    return (
        layer_output,
        input_grad,
        triple_grad,
        jnp.stack([query_sum, value_sum]),
        output_weight_grad,
        small_sums[0],
        small_sums[1],
        small_sums[2],
        expand_weight_grad,
        expand_bias_grad,
        reduce_weight_grad,
        small_sums[3],
        small_sums[4],
        small_sums[5],
    )


def solution(mesh):
    in_specs = (
        P("dp", "tensor"),
        P("dp", None),
        P(None, None, "tensor"),
        P(None, "tensor"),
        P("tensor", None),
        P("tensor"),
        P("tensor"),
        P("tensor"),
        P(None, "tensor"),
        P("tensor"),
        P("tensor", None),
        P("tensor"),
        P("tensor"),
        P("tensor"),
        P("dp", "tensor"),
    )
    out_specs = (
        P("dp", "tensor"),
        P("dp", "tensor"),
        P(None, None, "tensor"),
        P(None, "tensor"),
        P("tensor", None),
        P("tensor"),
        P("tensor"),
        P("tensor"),
        P(None, "tensor"),
        P("tensor"),
        P("tensor", None),
        P("tensor"),
        P("tensor"),
        P("tensor"),
    )
    return jax.shard_map(
        per_device, mesh=mesh, in_specs=in_specs, out_specs=out_specs, check_vma=False
    )
```
